1024 devices in a mesh: replica: 32 (over z, y_hi), fsdp: 32 (over x, y_lo, core).
Axes of the slice: x: 4, y: 8 (y_hi: 2, y_lo: 4; y = y_hi * 4 + y_lo), z: 16, core: 2. Of those that a mesh axis runs over, the one named last changes fastest.
Arguments:
- grad: bfloat16 [256, 512, 512], P('replica', 'fsdp'), may hold values from -180 to 180
- statistics: float32 [1024, 512, 256], P(('replica', 'fsdp')), may hold values from -2000 to 2000, as said below
- moment: float32 [1024, 256, 256], P(('replica', 'fsdp')), may hold values from 0.01 to 10
- assignment: int32 [256], P('replica'), may hold values from 0 to 15, as said below
- newton_steps: int32 [256], P('replica'), may hold values from 2 to 3
Outputs:
- direction: bfloat16 [32, 32, 256, 256], P(None, 'fsdp')
- new_statistics: float32 [1024, 512, 256], P(('replica', 'fsdp'))
- new_moment: float32 [1024, 256, 256], P(('replica', 'fsdp'))
The draws below stay inside these ranges and needn't reach their ends.
Inputs may be any that keep to these rules, and one draw needn't show every extreme that they name: `assignment`: for every replica group r, entries r * 8 to (r + 1) * 8 - 1 taken modulo 32 / 4 are a permutation of 0 to 7. `statistics`: the two factors that the column halves of each slot form are symmetric positive definite.
All inputs are finite; a program needn't handle non-finite values.
Results may differ from the reference program's by a relative error of at most 0.001.
Values may be sent and summed in bfloat16 or wider, within the bound.
A program may use at most 32 MiB of HBM per device.

```python
import math
import jax
import jax.numpy as jnp
from jax import lax

BS = 512
NEWTON_MAX = 3
NBLK = 256
N_REPLICA = 32
N_FSDP = 32


def draw_grad(key, part):
    key = jax.random.fold_in(key, 7)
    subkeys = jax.random.split(key, 3)
    noise_part = jnp.clip(jax.random.normal(subkeys[0], (NBLK, BS, BS), jnp.float32), -6.0, 6.0)
    row_scales = jnp.exp(jax.random.uniform(subkeys[1], (NBLK, BS, 1), jnp.float32, 0.0, 2.3026))
    col_scales = jnp.exp(jax.random.uniform(subkeys[2], (NBLK, 1, BS), jnp.float32, 0.0, 2.3026))
    block_rise = 3.0 ** (jnp.arange(NBLK, dtype=jnp.float32) / max(NBLK - 1, 1))
    return (noise_part * row_scales * col_scales * block_rise[:, None, None] * 0.1).astype(jnp.bfloat16)


def draw_statistics(key, part):
    key = jax.random.fold_in(key, 11)
    subkeys = jax.random.split(key, 2)
    scales = jnp.exp(jax.random.uniform(subkeys[0], (NBLK, 2, BS), jnp.float32, 2.9957, 7.6009))
    raw_coupling = jax.random.uniform(subkeys[1], (NBLK, 2, BS, BS), jnp.float32, -1.0, 1.0)
    coupling = 0.45 * (raw_coupling + jnp.swapaxes(raw_coupling, 2, 3)) / BS
    identity = jnp.eye(BS, dtype=jnp.float32)
    pattern = identity + coupling * (1.0 - identity)
    full_factors = jnp.sqrt(scales[:, :, :, None] * scales[:, :, None, :]) * pattern
    halves = full_factors.reshape(NBLK, 2, BS, 2, BS // 2).transpose(0, 1, 3, 2, 4)
    return halves.reshape(4 * NBLK, BS, BS // 2)


def draw_assignment(key, part):
    key = jax.random.fold_in(key, 5)
    per_group = N_FSDP // 4
    subkeys = jax.random.split(key, N_REPLICA + 1)
    orders = jax.vmap(lambda subkey: jax.random.permutation(subkey, per_group))(subkeys[:N_REPLICA])
    orders = orders.reshape(NBLK).astype(jnp.int32)
    flags = (jax.random.permutation(subkeys[N_REPLICA], NBLK) % 2).astype(jnp.int32)
    slots = jnp.arange(NBLK, dtype=jnp.int32)
    first_group = slots < per_group
    second_group = (slots >= per_group) & (slots < 2 * per_group)
    flags = jnp.where(first_group & (orders == per_group - 1), 1, flags)
    flags = jnp.where(second_group & (orders == 0), 0, flags)
    return (orders + per_group * flags).astype(jnp.int32)


def with_ends(result, rng, least, top_value):
    extent = result.shape
    index_at = [jax.random.randint(jax.random.fold_in(rng, axis), (), 0, extent[axis]) for axis in range(len(extent))]
    result = result.at[tuple(index_at)].set(least)
    longest = extent.index(max(extent))
    index_at[longest] = (index_at[longest] + 1) % extent[longest]
    return result.at[tuple(index_at)].set(top_value)


def shard_levels(rng, extent, cuts, least, largest):
    loudness = 1.0
    for dim, parts in cuts:
        draws = jax.random.uniform(jax.random.fold_in(jax.random.fold_in(rng, 6), dim), (parts,), jnp.float32, least / len(cuts), largest / len(cuts))
        loudness = loudness * jnp.repeat(jnp.exp(draws), extent[dim] // parts).reshape((-1,) + (1,) * (len(extent) - 1 - dim))
    return loudness


def setup_inputs(seed: int = 0) -> dict:
    keys = jax.random.split(jax.random.key(seed), 6)
    grad = draw_grad(jax.random.fold_in(keys[5], 71), 0)
    statistics = draw_statistics(jax.random.fold_in(keys[5], 71), 0)
    moment = jnp.clip(jnp.exp(math.log(10.0) - 6.9077553 * jax.random.uniform(keys[2], (4 * NBLK, BS // 2, BS // 2), jnp.float32) ** shard_levels(keys[2], (4 * NBLK, BS // 2, BS // 2), ((0, 1024),), -0.2, 0.2)), 0.01, 10.0)
    assignment = draw_assignment(jax.random.fold_in(keys[5], 71), 0)
    newton_steps = with_ends(jax.random.randint(keys[4], (NBLK,), 2, NEWTON_MAX + 1), jax.random.fold_in(keys[4], 1), 2, NEWTON_MAX).astype(jnp.int32)
    return dict(grad=grad, statistics=statistics, moment=moment, assignment=assignment, newton_steps=newton_steps)


highest = lax.Precision.HIGHEST

def product(left_part, right_part):
    return jnp.dot(left_part, right_part, precision=highest, preferred_element_type=jnp.float32)

def inverse_root(factor, newton_count):
    eye_full = jnp.eye(factor.shape[0], dtype=jnp.float32)
    frobenius = jnp.sqrt(jnp.sum(factor * factor) + 1e-06)
    iterate = factor / frobenius
    root_full = eye_full * frobenius ** (-0.25)
    for newton_step in range(NEWTON_MAX):
        tangent = (5.0 * eye_full - iterate) * 0.25
        advanced = product(tangent, root_full)
        square_full = product(tangent, tangent)
        next_iterate = product(square_full, product(square_full, iterate))
        keep_step = newton_step < newton_count
        root_full = jnp.where(keep_step, advanced, root_full)
        iterate = jnp.where(keep_step, next_iterate, iterate)
    return root_full

def reference(grad, statistics, moment, assignment, newton_steps):
    per_group = N_FSDP // 4
    half_width = BS // 2
    corners = ((0, 0), (1, 1), (0, 1), (1, 0))

    def one_slot(slot_index):
        group_index = slot_index // per_group
        entry = assignment[slot_index].astype(jnp.int32)
        block_id = (group_index * per_group + entry % per_group).astype(jnp.int32)
        flipped = entry // per_group
        raw_block = lax.dynamic_index_in_dim(grad, block_id, 0, keepdims=False)
        gradient_block = jnp.where(flipped == 1, raw_block.T, raw_block)
        newton_count = lax.dynamic_index_in_dim(newton_steps, block_id, 0, keepdims=False)
        old_halves = lax.dynamic_slice_in_dim(statistics, slot_index * 4, 4, 0)
        left_old = jnp.concatenate([old_halves[0], old_halves[1]], axis=1)
        right_old = jnp.concatenate([old_halves[2], old_halves[3]], axis=1)
        left_factor = 0.9 * left_old + 0.1 * jnp.dot(gradient_block, gradient_block.T, preferred_element_type=jnp.float32)
        right_factor = 0.9 * right_old + 0.1 * jnp.dot(gradient_block.T, gradient_block, preferred_element_type=jnp.float32)
        left_root = inverse_root(left_factor, newton_count)
        right_root = inverse_root(right_factor, newton_count)
        block_float = gradient_block.astype(jnp.float32)
        shaped = product(product(left_root.T, block_float), right_root)
        old_moments = lax.dynamic_slice_in_dim(moment, slot_index * 4, 4, 0)
        adam_sq = jnp.zeros((), jnp.float32)
        fresh_list = []
        pieces = []
        for member in range(4):
            row_half, col_half = corners[member]
            grad_quarter = block_float[row_half * half_width:(row_half + 1) * half_width, col_half * half_width:(col_half + 1) * half_width]
            fresh_moment = 0.95 * old_moments[member] + 0.05 * grad_quarter * grad_quarter
            adam_step = grad_quarter / (jnp.sqrt(fresh_moment) + 1e-08)
            adam_sq = adam_sq + jnp.sum(adam_step * adam_step)
            fresh_list.append(fresh_moment)
            pieces.append(shaped[row_half * half_width:(row_half + 1) * half_width, col_half * half_width:(col_half + 1) * half_width])
        graft_scale = jnp.sqrt(adam_sq / (BS * BS)) / jnp.sqrt(jnp.mean(shaped * shaped) + 1e-12)
        direction = jnp.stack([(graft_scale * piece).astype(jnp.bfloat16) for piece in pieces])
        new_stats = jnp.stack([left_factor[:, :half_width], left_factor[:, half_width:], right_factor[:, :half_width], right_factor[:, half_width:]])
        return (direction, new_stats, jnp.stack(fresh_list))
    direction, new_stats, new_moments = lax.map(one_slot, jnp.arange(NBLK, dtype=jnp.int32))
    direction = direction.reshape(N_REPLICA, N_FSDP, half_width, half_width)
    new_stats = new_stats.reshape(4 * NBLK, BS, half_width)
    new_moments = new_moments.reshape(4 * NBLK, half_width, half_width)
    return (direction, new_stats, new_moments)
```

```python
import functools

import jax
import jax.numpy as jnp
from jax import lax
from jax.experimental import pallas as pl
from jax.experimental.pallas import tpu as pltpu
from jax.sharding import PartitionSpec as P

MESH = pl.DeviceIdType.MESH


def make_plan(cross, chunks, tz=2.95, ty=6.2, lz=1.6, ly=2.6):
    routes = {}
    def add(a, s, b): routes.setdefault(a, []).append((s, b))
    def norm(d): return d if d <= 8 else d - 16
    half = chunks // 2
    for c in range(chunks):
        for d in range(0, 7): add((0, d, c), '+', (0, d + 1, c))
        for d in range(0, -7, -1): add((0, d, c), '-', (0, d - 1, c))
        if c < half: add((0, 7, c), '+', (0, 8, c))
        else: add((0, -7, c), '-', (0, 8, c))
        for d in cross: add((0, d, c), 'y', (1, d, c))
        cs = sorted(x % 16 for x in cross)
        flip = 0
        for i, a in enumerate(cs):
            b = cs[(i + 1) % len(cs)]
            if b <= a: b += 16
            n = b - a - 1
            left = n // 2; right = n // 2
            if n % 2:
                if (c < half) : left += 1
                else: right += 1
            for j in range(left): add((1, norm((a + j) % 16), c), '+', (1, norm((a + j + 1) % 16), c))
            for j in range(right): add((1, norm((b - j) % 16), c), '-', (1, norm((b - j - 1) % 16), c))
    import functools
    cost = {'+': tz / chunks + lz, '-': tz / chunks + lz, 'y': ty / chunks + ly}
    @functools.lru_cache(None)
    def rem(item):
        return max([cost[s] + rem(b) for s, b in routes.get(item, [])], default=0)
    dur = {'+': tz / chunks, '-': tz / chunks, 'y': ty / chunks}
    lat = {'+': lz, '-': lz, 'y': ly}
    free = {'+': 0., '-': 0., 'y': 0.}
    ready = {'+': [], '-': [], 'y': []}
    def arrive(item, t):
        for s, b in routes.get(item, []):
            ready[s].append((t, item, b))
    for c in range(chunks): arrive((0, 0, c), 0.0)
    order = []; end = 0
    while any(ready.values()):
        best = None
        for s in ready:
            if not ready[s]: continue
            t = max(free[s], min(r[0] for r in ready[s]))
            if best is None or t < best[0]: best = (t, s)
        t, s = best
        cand = [r for r in ready[s] if r[0] <= t + 1e-9]
        cand.sort(key=lambda r: (-(cost[s] + rem(r[2])), r[0], r[1]))
        r = cand[0]; ready[s].remove(r)
        free[s] = t + dur[s]
        order.append((t, s, r[1], r[2]))
        ta = t + dur[s] + lat[s]
        end = max(end, ta)
        arrive(r[2], ta)
    recvd = {}
    for t, s, a, b in order:
        assert b not in recvd, b
        recvd[b] = 1
    assert len(recvd) == 31 * chunks, len(recvd)
    nz = {s: sum(1 for o in order if o[1] == s) / chunks for s in '+-y'}
    return order, end, nz


def split(value):
    high = value.astype(jnp.bfloat16)
    return high, (value - high.astype(jnp.float32)).astype(jnp.bfloat16)


def dot(left, right):
    return jnp.dot(left, right, preferred_element_type=jnp.float32)


def dot_nt(left, right):
    return lax.dot_general(left, right, (((1,), (1,)), ((), ())), preferred_element_type=jnp.float32)


def dot_3(left_high, left_low, right_high, right_low):
    return dot(left_high, right_high) + (dot(left_high, right_low) + dot(left_low, right_high))


def shifted(rows, first_row, width):
    row = lax.broadcasted_iota(jnp.int32, rows.shape, 0) + first_row
    column = lax.broadcasted_iota(jnp.int32, rows.shape, 1)
    return jnp.where(row == column, 1.25, 0.0) - 0.25 * rows


def step_kernel(
    order,
    chunks,
    assign_hbm,
    newton_hbm,
    grad_hbm,
    stat_ref,
    moment_hbm,
    dir_ref,
    new_stat_ref,
    new_moment_ref,
    assign_ref,
    newton_ref,
    grad_ref,
    own_half,
    moment_ref,
    outgoing,
    block,
    block_turned,
    old,
    factor,
    core_grad,
    t_high,
    t_low,
    m_high,
    m_low,
    s_high,
    s_low,
    u_high,
    u_low,
    sent_root,
    other_root,
    quarter_ref,
    sums,
    own_direction,
    input_sem,
    output_sem,
    grad_send,
    grad_recv,
    pass_send,
    pass_recv,
    old_send,
    old_pass,
    old_recv,
    old_local,
    root_send,
    root_recv,
    sum_send,
    sum_recv,
    dir_send,
    dir_recv,
    dir_local,
):
    replica, fsdp = lax.axis_index("replica"), lax.axis_index("fsdp")
    z, y_high = replica // 2, lax.rem(replica, 2)
    chip, core = fsdp // 2, lax.rem(fsdp, 2)
    slot, side = chip // 2, lax.rem(chip, 2)
    member = lax.rem(fsdp, 4)
    twin = (replica, chip * 2 + 1 - core)
    beside = (replica, slot * 4 + (1 - side) * 2 + side)
    upward = (lax.rem(z + 1, 16) * 2 + y_high, fsdp)
    downward = (lax.rem(z + 15, 16) * 2 + y_high, fsdp)
    across = (z * 2 + 1 - y_high, fsdp)

    def same_core(distance):
        return (replica, lax.rem(chip + distance, 16) * 2 + core)

    def remote(source, target, send_sem, recv_sem, device):
        return pltpu.make_async_remote_copy(
            src_ref=source,
            dst_ref=target,
            send_sem=send_sem,
            recv_sem=recv_sem,
            device_id=device,
            device_id_type=MESH,
        )

    pairs = (
        (assign_hbm, assign_ref),
        (grad_hbm, grad_ref),
        (newton_hbm, newton_ref),
        (stat_ref.at[0], own_half),
        (moment_hbm.at[0], moment_ref),
    )
    inputs = [pltpu.make_async_copy(source, target, input_sem.at[i]) for i, (source, target) in enumerate(pairs)]
    for copy in inputs:
        copy.start()
    barrier = pltpu.get_barrier_semaphore()
    diagonal = (replica, slot * 4 + (1 - side) * 2 + (1 - core))
    greeted = [same_core(distance) for distance in range(1, 16)] + [twin, diagonal, upward, downward, across]
    for device in greeted:
        pl.semaphore_signal(barrier, inc=1, device_id=device, device_id_type=MESH)
    inputs[0].wait()
    inputs[1].wait()
    for target_slot in range(8):
        outgoing[target_slot] = grad_ref[lax.rem(assign_ref[target_slot], 8)]
    block[chip, core] = outgoing[slot]
    pl.semaphore_wait(barrier, len(greeted))

    grad_copies = []
    for distance in range(1, 16):
        target = lax.rem(chip + distance, 16)
        copy = remote(
            outgoing.at[target // 2],
            block.at[chip, core],
            grad_send.at[distance],
            grad_recv.at[distance],
            same_core(distance),
        )
        copy.start()
        grad_copies.append(copy)

    def old_piece(number):
        half, first = ((0, 0), (0, 256), (1, 256))[number]
        source = stat_ref.at[0, pl.ds(first, 256), :]
        here = old.at[number]
        return (
            half,
            remote(source, here, old_send.at[number], old_recv.at[number], beside),
            remote(source, here, old_pass.at[number], old_recv.at[number], twin),
            pltpu.make_async_copy(source, here, old_local.at[number]),
        )

    for number in range(3):
        half, to_beside, to_twin, to_self = old_piece(number)

        @pl.when(core == half)
        def _():
            to_beside.start()

        @pl.when((core == half) & (core == side))
        def _():
            to_self.start()

        @pl.when((core == half) & (core != side))
        def _():
            to_twin.start()

    pass_copies = []
    for distance in range(16):
        source = lax.rem(chip + 16 - distance, 16)
        if distance > 0:
            grad_copies[distance - 1].wait_recv()
        rows = block.at[source, core]
        copy = remote(rows, rows, pass_send.at[distance], pass_recv.at[distance], twin)
        copy.start()
        pass_copies.append(copy)
    for copy in pass_copies:
        copy.wait_recv()

    taken = assign_ref[slot]
    received = block[...].reshape(512, 512)
    row = lax.broadcasted_iota(jnp.int32, (512, 512), 0)
    column = lax.broadcasted_iota(jnp.int32, (512, 512), 1)
    identity = jnp.where(row == column, 1.0, 0.0).astype(jnp.bfloat16)
    flipped = dot_nt(identity, received)
    block_turned[...] = flipped.astype(jnp.bfloat16)

    def oriented(which):
        weight = lax.rem(taken // 8 + which, 2).astype(jnp.float32)
        plain = block[...].reshape(512, 512).astype(jnp.float32)
        return (plain * (1.0 - weight) + block_turned[...].astype(jnp.float32) * weight).astype(jnp.bfloat16)

    core_grad[...] = oriented(core)
    grams = [dot_nt(core_grad[pl.ds(part * 256, 256), :], core_grad[...]) for part in range(2)]
    for number in range(3):
        half, to_beside, to_twin, to_self = old_piece(number)
        local = (core == half) & (core == side)

        @pl.when(local)
        def _():
            to_self.wait()

        @pl.when(jnp.logical_not(local))
        def _():
            to_beside.wait_recv()

    lower = old[1]
    quarters = ((old[0], lower.T), (lower, old[2]))
    squares = jnp.zeros((1, 1), jnp.float32)
    for part in range(2):
        rows = pl.ds(part * 256, 256)
        for half in range(2):
            entry = 0.9 * quarters[part][half] + 0.1 * grams[part][:, half * 256 : (half + 1) * 256]
            factor[rows, pl.ds(half * 256, 256)] = entry
            squares = squares + jnp.sum(entry * entry, keepdims=True)
    norm = jnp.sqrt(squares + 1e-06)
    inverse = 1.0 / norm
    scale = lax.rsqrt(jnp.sqrt(norm))

    for part in range(2):
        rows = pl.ds(part * 256, 256)
        iterate = factor[rows, :] * inverse
        m_high[rows, :], m_low[rows, :] = split(iterate)
        tangent = shifted(iterate, part * 256, 512)
        factor[rows, :] = tangent
        t_high[rows, :], t_low[rows, :] = split(tangent)
    for part in range(2):
        rows = pl.ds(part * 256, 256)
        s_high[rows, :], s_low[rows, :] = split(dot_3(t_high[rows, :], t_low[rows, :], t_high[...], t_low[...]))
    for part in range(2):
        rows = pl.ds(part * 256, 256)
        u_high[rows, :], u_low[rows, :] = split(dot_3(s_high[rows, :], s_low[rows, :], m_high[...], m_low[...]))
    for part in range(2):
        rows = pl.ds(part * 256, 256)
        iterate = dot_3(s_high[rows, :], s_low[rows, :], u_high[...], u_low[...])
        m_high[rows, :], m_low[rows, :] = split(iterate)
        t_high[rows, :], t_low[rows, :] = split(shifted(iterate, part * 256, 512))

    for part in range(2):
        rows = pl.ds(part * 256, 256)
        s_high[rows, :], s_low[rows, :] = split(dot_3(t_high[rows, :], t_low[rows, :], t_high[...], t_low[...]))
    inputs[2].wait()
    steps = newton_ref[lax.rem(taken, 8)]

    def root_rows(first):
        start = factor[pl.ds(pl.multiple_of(first * 256, 256), 256), :]
        second = dot_3(*split(start), t_high[...], t_low[...])
        third = dot_3(*split(second), m_high[...], m_low[...])
        third = dot_3(*split(third), s_high[...], s_low[...])
        third = dot_3(*split(third), s_high[...], s_low[...])
        third = 1.25 * second - 0.25 * third
        return scale * jnp.where(jnp.full((256, 512), steps) > 2, third, second)

    own = core * (1 - side)
    sent_root[...] = root_rows(1 - own)
    root_copy = remote(sent_root, other_root, root_send, root_recv, twin)
    root_copy.start()
    root_high, root_low = split(root_rows(own))
    shaped = dot(root_high, core_grad[...]) + dot(root_low, core_grad[...])
    u_high[0:256, :], u_low[0:256, :] = split(shaped)

    first_row = pl.multiple_of(own * 256, 256)
    first_column = pl.multiple_of((side * (1 - core) + core) * 256, 256)
    quarter_ref[...] = core_grad[pl.ds(first_row, 256), pl.ds(first_column, 256)].astype(jnp.float32)

    @pl.when(core == 1)
    def _():
        quarter_ref[...] = quarter_ref[...].T

    inputs[4].wait()
    entries = quarter_ref[...]
    fresh = 0.95 * moment_ref[...] + 0.05 * entries * entries
    moment_ref[...] = fresh
    adam = entries / (jnp.sqrt(fresh) + 1e-08)
    adam_sum = jnp.sum(adam * adam, keepdims=True)
    moment_out = pltpu.make_async_copy(moment_ref, new_moment_ref.at[0], output_sem.at[0])
    moment_out.start()
    root_copy.wait_recv()
    root_high, root_low = split(other_root[...])
    shaped_high, shaped_low = u_high[0:256, :], u_low[0:256, :]
    quarter = dot_nt(shaped_high, root_high) + (dot_nt(shaped_high, root_low) + dot_nt(shaped_low, root_high))
    quarter_ref[...] = quarter
    quarter_sum = jnp.sum(quarter * quarter, keepdims=True)
    line = lax.broadcasted_iota(jnp.int32, (8, 128), 0)
    sums[member] = jnp.where(line == 0, adam_sum, quarter_sum)
    sum_copies = []
    for distance in range(1, 4):
        device = (replica, slot * 4 + lax.rem(member + distance, 4))
        copy = remote(sums.at[member], sums.at[member], sum_send.at[distance], sum_recv.at[distance], device)
        copy.start()
        sum_copies.append(copy)

    @pl.when(core == 1)
    def _():
        quarter_ref[...] = quarter_ref[...].T

    for copy in sum_copies:
        copy.wait_recv()
    total = (sums[0] + sums[1]) + (sums[2] + sums[3])
    mean = total * (1.0 / (512 * 512))
    graft = jnp.sqrt(mean[0:1, 0:1]) / jnp.sqrt(mean[1:2, 0:1] + 1e-12)
    own_direction[...] = (graft * quarter_ref[...]).astype(jnp.bfloat16)

    keep = pltpu.make_async_copy(own_direction, dir_ref.at[replica, 0], dir_local)
    keep.start()
    height = 256 // chunks
    numbers = {send[3]: number for number, send in enumerate(order)}
    ways = {"+": upward, "-": downward, "y": across}

    def place(item):
        kind, distance, chunk = item
        column_of = y_high if kind == 0 else 1 - y_high
        return dir_ref.at[lax.rem(z + 16 - distance, 16) * 2 + column_of, 0, pl.ds(chunk * height, height), :]

    arrived = {(0, 0, chunk) for chunk in range(chunks)}

    def await_item(item):
        if item not in arrived:
            arrived.add(item)
            remote(place(item), place(item), dir_send.at[0], dir_recv.at[numbers[item]], upward).wait_recv()

    dir_copies = []
    stat_out = pltpu.make_async_copy(own_half, new_stat_ref.at[0], output_sem.at[1])
    for number, (_, way, item, landing) in enumerate(order):
        if number == 3 * chunks:
            inputs[3].wait()
            block_turned[...] = oriented(side)
            half_rows = block_turned[pl.ds(pl.multiple_of(core * 256, 256), 256), :]
            own_half[...] = 0.9 * own_half[...] + 0.1 * dot_nt(block_turned[...], half_rows)
            stat_out.start()
        await_item(item)
        source = place(item)
        if item[:2] == (0, 0):
            source = own_direction.at[pl.ds(item[2] * height, height), :]
        copy = remote(source, place(item), dir_send.at[number], dir_recv.at[number], ways[way])
        copy.start()
        dir_copies.append(copy)
    for item in numbers:
        await_item(item)
    keep.wait()
    moment_out.wait()
    stat_out.wait()
    root_copy.wait_send()
    for number in range(3):
        half, to_beside, to_twin, to_self = old_piece(number)

        @pl.when(core == half)
        def _():
            to_beside.wait_send()

        @pl.when((core == half) & (core != side))
        def _():
            to_twin.wait_send()

    for copy in grad_copies + pass_copies + sum_copies + dir_copies:
        copy.wait_send()


CROSSINGS = (0, 3, 6, -6, -3)
CHUNKS = 2


def on_device(grad, statistics, moment, assignment, newton_steps):
    order = make_plan(CROSSINGS, CHUNKS)[0]
    anywhere = pl.BlockSpec(memory_space=pl.ANY)
    wide_16 = pltpu.VMEM((512, 512), jnp.bfloat16)
    wide_32 = pltpu.VMEM((512, 512), jnp.float32)
    dma = pltpu.SemaphoreType.DMA
    return pl.pallas_call(
        functools.partial(step_kernel, order, CHUNKS),
        out_shape=(
            jax.ShapeDtypeStruct((32, 1, 256, 256), jnp.bfloat16),
            jax.ShapeDtypeStruct((1, 512, 256), jnp.float32),
            jax.ShapeDtypeStruct((1, 256, 256), jnp.float32),
        ),
        in_specs=[anywhere] * 5,
        out_specs=(anywhere, anywhere, anywhere),
        scratch_shapes=[
            pltpu.SMEM((8,), jnp.int32),
            pltpu.SMEM((8,), jnp.int32),
            pltpu.VMEM((8, 16, 512), jnp.bfloat16),
            pltpu.VMEM((512, 256), jnp.float32),
            pltpu.VMEM((256, 256), jnp.float32),
            pltpu.VMEM((8, 16, 512), jnp.bfloat16),
            pltpu.VMEM((16, 2, 16, 512), jnp.bfloat16),
            wide_16,
            pltpu.VMEM((3, 256, 256), jnp.float32),
            wide_32,
        ]
        + [wide_16] * 9
        + [
            pltpu.VMEM((256, 512), jnp.float32),
            pltpu.VMEM((256, 512), jnp.float32),
            pltpu.VMEM((256, 256), jnp.float32),
            pltpu.VMEM((4, 8, 128), jnp.float32),
            pltpu.VMEM((256, 256), jnp.bfloat16),
            dma((5,)),
            dma((2,)),
            dma((16,)),
            dma((16,)),
            dma((16,)),
            dma((16,)),
            dma((3,)),
            dma((3,)),
            dma((3,)),
            dma((3,)),
            dma,
            dma,
            dma((4,)),
            dma((4,)),
            dma((len(order),)),
            dma((len(order),)),
            dma,
        ],
        compiler_params=pltpu.CompilerParams(
            collective_id=0, has_side_effects=True, vmem_limit_bytes=60 << 20
        ),
        name="shampoo_step",
    )(assignment, newton_steps, grad, statistics, moment)


def solution(mesh):
    placed = (
        P("replica", "fsdp", None),
        P(("replica", "fsdp"), None, None),
        P(("replica", "fsdp"), None, None),
        P("replica"),
        P("replica"),
    )
    return jax.shard_map(
        on_device,
        mesh=mesh,
        in_specs=placed,
        out_specs=(
            P(None, "fsdp", None, None),
            P(("replica", "fsdp"), None, None),
            P(("replica", "fsdp"), None, None),
        ),
        check_vma=False,
    )
```

```python
import functools

import jax
import jax.numpy as jnp
from jax import lax
from jax.experimental import pallas as pl
from jax.experimental.pallas import tpu as pltpu
from jax.sharding import PartitionSpec as P

MESH = pl.DeviceIdType.MESH


def make_plan(cross, chunks, tz=2.95, ty=6.2, lz=1.6, ly=2.6):
    routes = {}
    def add(a, s, b): routes.setdefault(a, []).append((s, b))
    def norm(d): return d if d <= 8 else d - 16
    half = chunks // 2
    for c in range(chunks):
        for d in range(0, 7): add((0, d, c), '+', (0, d + 1, c))
        for d in range(0, -7, -1): add((0, d, c), '-', (0, d - 1, c))
        if c < half: add((0, 7, c), '+', (0, 8, c))
        else: add((0, -7, c), '-', (0, 8, c))
        for d in cross: add((0, d, c), 'y', (1, d, c))
        cs = sorted(x % 16 for x in cross)
        flip = 0
        for i, a in enumerate(cs):
            b = cs[(i + 1) % len(cs)]
            if b <= a: b += 16
            n = b - a - 1
            left = n // 2; right = n // 2
            if n % 2:
                if (c < half) : left += 1
                else: right += 1
            for j in range(left): add((1, norm((a + j) % 16), c), '+', (1, norm((a + j + 1) % 16), c))
            for j in range(right): add((1, norm((b - j) % 16), c), '-', (1, norm((b - j - 1) % 16), c))
    import functools
    cost = {'+': tz / chunks + lz, '-': tz / chunks + lz, 'y': ty / chunks + ly}
    @functools.lru_cache(None)
    def rem(item):
        return max([cost[s] + rem(b) for s, b in routes.get(item, [])], default=0)
    dur = {'+': tz / chunks, '-': tz / chunks, 'y': ty / chunks}
    lat = {'+': lz, '-': lz, 'y': ly}
    free = {'+': 0., '-': 0., 'y': 0.}
    ready = {'+': [], '-': [], 'y': []}
    def arrive(item, t):
        for s, b in routes.get(item, []):
            ready[s].append((t, item, b))
    for c in range(chunks): arrive((0, 0, c), 0.0)
    order = []; end = 0
    while any(ready.values()):
        best = None
        for s in ready:
            if not ready[s]: continue
            t = max(free[s], min(r[0] for r in ready[s]))
            if best is None or t < best[0]: best = (t, s)
        t, s = best
        cand = [r for r in ready[s] if r[0] <= t + 1e-9]
        cand.sort(key=lambda r: (-(cost[s] + rem(r[2])), r[0], r[1]))
        r = cand[0]; ready[s].remove(r)
        free[s] = t + dur[s]
        order.append((t, s, r[1], r[2]))
        ta = t + dur[s] + lat[s]
        end = max(end, ta)
        arrive(r[2], ta)
    recvd = {}
    for t, s, a, b in order:
        assert b not in recvd, b
        recvd[b] = 1
    assert len(recvd) == 31 * chunks, len(recvd)
    nz = {s: sum(1 for o in order if o[1] == s) / chunks for s in '+-y'}
    return order, end, nz


def split(value):
    high = value.astype(jnp.bfloat16)
    return high, (value - high.astype(jnp.float32)).astype(jnp.bfloat16)


def dot(left, right):
    return jnp.dot(left, right, preferred_element_type=jnp.float32)


def dot_nt(left, right):
    return lax.dot_general(left, right, (((1,), (1,)), ((), ())), preferred_element_type=jnp.float32)


def dot_3(left_high, left_low, right_high, right_low):
    return dot(left_high, right_high) + (dot(left_high, right_low) + dot(left_low, right_high))


def shifted(rows, first_row, width):
    row = lax.broadcasted_iota(jnp.int32, rows.shape, 0) + first_row
    column = lax.broadcasted_iota(jnp.int32, rows.shape, 1)
    return jnp.where(row == column, 1.25, 0.0) - 0.25 * rows


def step_kernel(
    order,
    chunks,
    assign_hbm,
    newton_hbm,
    grad_hbm,
    stat_ref,
    moment_hbm,
    dir_ref,
    new_stat_ref,
    new_moment_ref,
    assign_ref,
    newton_ref,
    grad_ref,
    own_half,
    moment_ref,
    outgoing,
    block,
    block_turned,
    old,
    factor,
    core_grad,
    t_high,
    t_low,
    m_high,
    m_low,
    s_high,
    s_low,
    u_high,
    u_low,
    sent_root,
    other_root,
    quarter_ref,
    sums,
    own_direction,
    input_sem,
    output_sem,
    grad_send,
    grad_recv,
    pass_send,
    pass_recv,
    old_send,
    old_pass,
    old_recv,
    old_local,
    root_send,
    root_recv,
    sum_send,
    sum_recv,
    dir_send,
    dir_recv,
    dir_local,
):
    replica, fsdp = lax.axis_index("replica"), lax.axis_index("fsdp")
    z, y_high = replica // 2, lax.rem(replica, 2)
    chip, core = fsdp // 2, lax.rem(fsdp, 2)
    slot, side = chip // 2, lax.rem(chip, 2)
    member = lax.rem(fsdp, 4)
    twin = (replica, chip * 2 + 1 - core)
    beside = (replica, slot * 4 + (1 - side) * 2 + side)
    upward = (lax.rem(z + 1, 16) * 2 + y_high, fsdp)
    downward = (lax.rem(z + 15, 16) * 2 + y_high, fsdp)
    across = (z * 2 + 1 - y_high, fsdp)

    def same_core(distance):
        return (replica, lax.rem(chip + distance, 16) * 2 + core)

    def remote(source, target, send_sem, recv_sem, device):
        return pltpu.make_async_remote_copy(
            src_ref=source,
            dst_ref=target,
            send_sem=send_sem,
            recv_sem=recv_sem,
            device_id=device,
            device_id_type=MESH,
        )

    pairs = (
        (assign_hbm, assign_ref),
        (grad_hbm, grad_ref),
        (newton_hbm, newton_ref),
        (stat_ref.at[0], own_half),
        (moment_hbm.at[0], moment_ref),
    )
    inputs = [pltpu.make_async_copy(source, target, input_sem.at[i]) for i, (source, target) in enumerate(pairs)]
    for copy in inputs:
        copy.start()
    barrier = pltpu.get_barrier_semaphore()
    diagonal = (replica, slot * 4 + (1 - side) * 2 + (1 - core))
    greeted = [same_core(distance) for distance in range(1, 16)] + [twin, diagonal, upward, downward, across]
    for device in greeted:
        pl.semaphore_signal(barrier, inc=1, device_id=device, device_id_type=MESH)
    inputs[0].wait()
    inputs[1].wait()
    for target_slot in range(8):
        outgoing[target_slot] = grad_ref[lax.rem(assign_ref[target_slot], 8)]
    block[chip, core] = outgoing[slot]
    pl.semaphore_wait(barrier, len(greeted))

    grad_copies = []
    for distance in range(1, 16):
        target = lax.rem(chip + distance, 16)
        copy = remote(
            outgoing.at[target // 2],
            block.at[chip, core],
            grad_send.at[distance],
            grad_recv.at[distance],
            same_core(distance),
        )
        copy.start()
        grad_copies.append(copy)

    def old_piece(number):
        half, first = ((0, 0), (0, 256), (1, 256))[number]
        source = stat_ref.at[0, pl.ds(first, 256), :]
        here = old.at[number]
        return (
            half,
            remote(source, here, old_send.at[number], old_recv.at[number], beside),
            remote(source, here, old_pass.at[number], old_recv.at[number], twin),
            pltpu.make_async_copy(source, here, old_local.at[number]),
        )

    for number in range(3):
        half, to_beside, to_twin, to_self = old_piece(number)

        @pl.when(core == half)
        def _():
            to_beside.start()

        @pl.when((core == half) & (core == side))
        def _():
            to_self.start()

        @pl.when((core == half) & (core != side))
        def _():
            to_twin.start()

    pass_copies = []
    for distance in range(16):
        source = lax.rem(chip + 16 - distance, 16)
        if distance > 0:
            grad_copies[distance - 1].wait_recv()
        rows = block.at[source, core]
        copy = remote(rows, rows, pass_send.at[distance], pass_recv.at[distance], twin)
        copy.start()
        pass_copies.append(copy)
    for copy in pass_copies:
        copy.wait_recv()

    taken = assign_ref[slot]
    received = block[...].reshape(512, 512)
    row = lax.broadcasted_iota(jnp.int32, (512, 512), 0)
    column = lax.broadcasted_iota(jnp.int32, (512, 512), 1)
    identity = jnp.where(row == column, 1.0, 0.0).astype(jnp.bfloat16)
    flipped = dot_nt(identity, received)
    block_turned[...] = flipped.astype(jnp.bfloat16)

    def oriented(which):
        weight = lax.rem(taken // 8 + which, 2).astype(jnp.float32)
        plain = block[...].reshape(512, 512).astype(jnp.float32)
        return (plain * (1.0 - weight) + block_turned[...].astype(jnp.float32) * weight).astype(jnp.bfloat16)

    core_grad[...] = oriented(core)
    grams = [dot_nt(core_grad[pl.ds(part * 256, 256), :], core_grad[...]) for part in range(2)]
    for number in range(3):
        half, to_beside, to_twin, to_self = old_piece(number)
        local = (core == half) & (core == side)

        @pl.when(local)
        def _():
            to_self.wait()

        @pl.when(jnp.logical_not(local))
        def _():
            to_beside.wait_recv()

    lower = old[1]
    quarters = ((old[0], lower.T), (lower, old[2]))
    squares = jnp.zeros((1, 1), jnp.float32)
    for part in range(2):
        rows = pl.ds(part * 256, 256)
        for half in range(2):
            entry = 0.9 * quarters[part][half] + 0.1 * grams[part][:, half * 256 : (half + 1) * 256]
            factor[rows, pl.ds(half * 256, 256)] = entry
            squares = squares + jnp.sum(entry * entry, keepdims=True)
    norm = jnp.sqrt(squares + 1e-06)
    inverse = 1.0 / norm
    scale = lax.rsqrt(jnp.sqrt(norm))

    for part in range(2):
        rows = pl.ds(part * 256, 256)
        iterate = factor[rows, :] * inverse
        m_high[rows, :], m_low[rows, :] = split(iterate)
        tangent = shifted(iterate, part * 256, 512)
        factor[rows, :] = tangent
        t_high[rows, :], t_low[rows, :] = split(tangent)
    for part in range(2):
        rows = pl.ds(part * 256, 256)
        s_high[rows, :], s_low[rows, :] = split(dot_3(t_high[rows, :], t_low[rows, :], t_high[...], t_low[...]))
    for part in range(2):
        rows = pl.ds(part * 256, 256)
        u_high[rows, :], u_low[rows, :] = split(dot_3(s_high[rows, :], s_low[rows, :], m_high[...], m_low[...]))
    for part in range(2):
        rows = pl.ds(part * 256, 256)
        iterate = dot_3(s_high[rows, :], s_low[rows, :], u_high[...], u_low[...])
        m_high[rows, :], m_low[rows, :] = split(iterate)
        t_high[rows, :], t_low[rows, :] = split(shifted(iterate, part * 256, 512))

    for part in range(2):
        rows = pl.ds(part * 256, 256)
        s_high[rows, :], s_low[rows, :] = split(dot_3(t_high[rows, :], t_low[rows, :], t_high[...], t_low[...]))
    inputs[2].wait()
    steps = newton_ref[lax.rem(taken, 8)]

    def root_rows(first):
        start = factor[pl.ds(pl.multiple_of(first * 256, 256), 256), :]
        second = dot_3(*split(start), t_high[...], t_low[...])
        third = dot_3(*split(second), m_high[...], m_low[...])
        third = dot_3(*split(third), s_high[...], s_low[...])
        third = dot_3(*split(third), s_high[...], s_low[...])
        third = 1.25 * second - 0.25 * third
        return scale * jnp.where(jnp.full((256, 512), steps) > 2, third, second)

    own = core * (1 - side)
    sent_root[...] = root_rows(1 - own)
    root_copy = remote(sent_root, other_root, root_send, root_recv, twin)
    root_copy.start()
    root_high, root_low = split(root_rows(own))
    shaped = dot(root_high, core_grad[...]) + dot(root_low, core_grad[...])
    u_high[0:256, :], u_low[0:256, :] = split(shaped)

    first_row = pl.multiple_of(own * 256, 256)
    first_column = pl.multiple_of((side * (1 - core) + core) * 256, 256)
    quarter_ref[...] = core_grad[pl.ds(first_row, 256), pl.ds(first_column, 256)].astype(jnp.float32)

    @pl.when(core == 1)
    def _():
        quarter_ref[...] = quarter_ref[...].T

    inputs[4].wait()
    entries = quarter_ref[...]
    fresh = 0.95 * moment_ref[...] + 0.05 * entries * entries
    moment_ref[...] = fresh
    adam = entries / (jnp.sqrt(fresh) + 1e-08)
    adam_sum = jnp.sum(adam * adam, keepdims=True)
    moment_out = pltpu.make_async_copy(moment_ref, new_moment_ref.at[0], output_sem.at[0])
    moment_out.start()
    root_copy.wait_recv()
    root_high, root_low = split(other_root[...])
    shaped_high, shaped_low = u_high[0:256, :], u_low[0:256, :]
    quarter = dot_nt(shaped_high, root_high) + (dot_nt(shaped_high, root_low) + dot_nt(shaped_low, root_high))
    quarter_ref[...] = quarter
    quarter_sum = jnp.sum(quarter * quarter, keepdims=True)
    line = lax.broadcasted_iota(jnp.int32, (8, 128), 0)
    sums[member] = jnp.where(line == 0, adam_sum, quarter_sum)
    sum_copies = []
    for distance in range(1, 4):
        device = (replica, slot * 4 + lax.rem(member + distance, 4))
        copy = remote(sums.at[member], sums.at[member], sum_send.at[distance], sum_recv.at[distance], device)
        copy.start()
        sum_copies.append(copy)

    @pl.when(core == 1)
    def _():
        quarter_ref[...] = quarter_ref[...].T

    for copy in sum_copies:
        copy.wait_recv()
    total = (sums[0] + sums[1]) + (sums[2] + sums[3])
    mean = total * (1.0 / (512 * 512))
    graft = jnp.sqrt(mean[0:1, 0:1]) / jnp.sqrt(mean[1:2, 0:1] + 1e-12)
    own_direction[...] = (graft * quarter_ref[...]).astype(jnp.bfloat16)

    keep = pltpu.make_async_copy(own_direction, dir_ref.at[replica, 0], dir_local)
    keep.start()
    height = 256 // chunks
    numbers = {send[3]: number for number, send in enumerate(order)}
    ways = {"+": upward, "-": downward, "y": across}

    def place(item):
        kind, distance, chunk = item
        column_of = y_high if kind == 0 else 1 - y_high
        return dir_ref.at[lax.rem(z + 16 - distance, 16) * 2 + column_of, 0, pl.ds(chunk * height, height), :]

    arrived = {(0, 0, chunk) for chunk in range(chunks)}

    def await_item(item):
        if item not in arrived:
            arrived.add(item)
            remote(place(item), place(item), dir_send.at[0], dir_recv.at[numbers[item]], upward).wait_recv()

    dir_copies = []
    stat_out = pltpu.make_async_copy(own_half, new_stat_ref.at[0], output_sem.at[1])
    for number, (_, way, item, landing) in enumerate(order):
        if number == 3 * chunks:
            inputs[3].wait()
            block_turned[...] = oriented(side)
            half_rows = block_turned[pl.ds(pl.multiple_of(core * 256, 256), 256), :]
            own_half[...] = 0.9 * own_half[...] + 0.1 * dot_nt(block_turned[...], half_rows)
            stat_out.start()
        await_item(item)
        source = place(item)
        if item[:2] == (0, 0):
            source = own_direction.at[pl.ds(item[2] * height, height), :]
        copy = remote(source, place(item), dir_send.at[number], dir_recv.at[number], ways[way])
        copy.start()
        dir_copies.append(copy)
    for item in numbers:
        await_item(item)
    keep.wait()
    moment_out.wait()
    stat_out.wait()
    root_copy.wait_send()
    for number in range(3):
        half, to_beside, to_twin, to_self = old_piece(number)

        @pl.when(core == half)
        def _():
            to_beside.wait_send()

        @pl.when((core == half) & (core != side))
        def _():
            to_twin.wait_send()

    for copy in grad_copies + pass_copies + sum_copies + dir_copies:
        copy.wait_send()


CROSSINGS = (0, 3, 6, -6, -3)
CHUNKS = 2


def place_kernel(dir_ref, stat_ref, moment_ref, dir_out, stat_out, moment_out, sem):
    copies = [
        pltpu.make_async_copy(dir_ref.at[pl.ds(part * 8, 8)], dir_out.at[pl.ds(part * 8, 8)], sem.at[part])
        for part in range(4)
    ]
    copies.append(pltpu.make_async_copy(stat_ref, stat_out, sem.at[4]))
    copies.append(pltpu.make_async_copy(moment_ref, moment_out, sem.at[5]))
    for copy in copies:
        copy.start()
    for copy in copies:
        copy.wait()


def on_device(grad, statistics, moment, assignment, newton_steps):
    order = make_plan(CROSSINGS, CHUNKS)[0]
    anywhere = pl.BlockSpec(memory_space=pl.ANY)
    wide_16 = pltpu.VMEM((512, 512), jnp.bfloat16)
    wide_32 = pltpu.VMEM((512, 512), jnp.float32)
    dma = pltpu.SemaphoreType.DMA
    results = pl.pallas_call(
        functools.partial(step_kernel, order, CHUNKS),
        out_shape=(
            jax.ShapeDtypeStruct((32, 1, 256, 256), jnp.bfloat16),
            jax.ShapeDtypeStruct((1, 512, 256), jnp.float32),
            jax.ShapeDtypeStruct((1, 256, 256), jnp.float32),
        ),
        in_specs=[anywhere] * 5,
        out_specs=(anywhere, anywhere, anywhere),
        scratch_shapes=[
            pltpu.SMEM((8,), jnp.int32),
            pltpu.SMEM((8,), jnp.int32),
            pltpu.VMEM((8, 16, 512), jnp.bfloat16),
            pltpu.VMEM((512, 256), jnp.float32),
            pltpu.VMEM((256, 256), jnp.float32),
            pltpu.VMEM((8, 16, 512), jnp.bfloat16),
            pltpu.VMEM((16, 2, 16, 512), jnp.bfloat16),
            wide_16,
            pltpu.VMEM((3, 256, 256), jnp.float32),
            wide_32,
        ]
        + [wide_16] * 9
        + [
            pltpu.VMEM((256, 512), jnp.float32),
            pltpu.VMEM((256, 512), jnp.float32),
            pltpu.VMEM((256, 256), jnp.float32),
            pltpu.VMEM((4, 8, 128), jnp.float32),
            pltpu.VMEM((256, 256), jnp.bfloat16),
            dma((5,)),
            dma((2,)),
            dma((16,)),
            dma((16,)),
            dma((16,)),
            dma((16,)),
            dma((3,)),
            dma((3,)),
            dma((3,)),
            dma((3,)),
            dma,
            dma,
            dma((4,)),
            dma((4,)),
            dma((len(order),)),
            dma((len(order),)),
            dma,
        ],
        compiler_params=pltpu.CompilerParams(
            collective_id=0, has_side_effects=True, vmem_limit_bytes=24 << 20
        ),
        name="shampoo_step",
    )(*(pltpu.with_memory_space_constraint(x, pltpu.HBM) for x in (assignment, newton_steps, grad, statistics, moment)))
    return pl.pallas_call(
        place_kernel,
        out_shape=tuple(jax.ShapeDtypeStruct(result.shape, result.dtype) for result in results),
        in_specs=[anywhere] * 3,
        out_specs=[anywhere] * 3,
        scratch_shapes=[dma((6,))],
        compiler_params=pltpu.CompilerParams(vmem_limit_bytes=8 << 20),
        name="place_results",
    )(*results)


def solution(mesh):
    placed = (
        P("replica", "fsdp", None),
        P(("replica", "fsdp"), None, None),
        P(("replica", "fsdp"), None, None),
        P("replica"),
        P("replica"),
    )
    return jax.shard_map(
        on_device,
        mesh=mesh,
        in_specs=placed,
        out_specs=(
            P(None, "fsdp", None, None),
            P(("replica", "fsdp"), None, None),
            P(("replica", "fsdp"), None, None),
        ),
        check_vma=False,
    )
```

```python
import functools

import jax
import jax.numpy as jnp
from jax import lax
from jax.experimental import pallas as pl
from jax.experimental.pallas import tpu as pltpu
from jax.sharding import PartitionSpec as P

MESH = pl.DeviceIdType.MESH


def make_plan(cross, chunks, tz=2.95, ty=6.2, lz=1.6, ly=2.6):
    routes = {}
    def add(a, s, b): routes.setdefault(a, []).append((s, b))
    def norm(d): return d if d <= 8 else d - 16
    half = chunks // 2
    for c in range(chunks):
        for d in range(0, 7): add((0, d, c), '+', (0, d + 1, c))
        for d in range(0, -7, -1): add((0, d, c), '-', (0, d - 1, c))
        if c < half: add((0, 7, c), '+', (0, 8, c))
        else: add((0, -7, c), '-', (0, 8, c))
        for d in cross: add((0, d, c), 'y', (1, d, c))
        cs = sorted(x % 16 for x in cross)
        flip = 0
        for i, a in enumerate(cs):
            b = cs[(i + 1) % len(cs)]
            if b <= a: b += 16
            n = b - a - 1
            left = n // 2; right = n // 2
            if n % 2:
                if (c < half) : left += 1
                else: right += 1
            for j in range(left): add((1, norm((a + j) % 16), c), '+', (1, norm((a + j + 1) % 16), c))
            for j in range(right): add((1, norm((b - j) % 16), c), '-', (1, norm((b - j - 1) % 16), c))
    import functools
    cost = {'+': tz / chunks + lz, '-': tz / chunks + lz, 'y': ty / chunks + ly}
    @functools.lru_cache(None)
    def rem(item):
        return max([cost[s] + rem(b) for s, b in routes.get(item, [])], default=0)
    dur = {'+': tz / chunks, '-': tz / chunks, 'y': ty / chunks}
    lat = {'+': lz, '-': lz, 'y': ly}
    free = {'+': 0., '-': 0., 'y': 0.}
    ready = {'+': [], '-': [], 'y': []}
    def arrive(item, t):
        for s, b in routes.get(item, []):
            ready[s].append((t, item, b))
    for c in range(chunks): arrive((0, 0, c), 0.0)
    order = []; end = 0
    while any(ready.values()):
        best = None
        for s in ready:
            if not ready[s]: continue
            t = max(free[s], min(r[0] for r in ready[s]))
            if best is None or t < best[0]: best = (t, s)
        t, s = best
        cand = [r for r in ready[s] if r[0] <= t + 1e-9]
        cand.sort(key=lambda r: (-(cost[s] + rem(r[2])), r[0], r[1]))
        r = cand[0]; ready[s].remove(r)
        free[s] = t + dur[s]
        order.append((t, s, r[1], r[2]))
        ta = t + dur[s] + lat[s]
        end = max(end, ta)
        arrive(r[2], ta)
    recvd = {}
    for t, s, a, b in order:
        assert b not in recvd, b
        recvd[b] = 1
    assert len(recvd) == 31 * chunks, len(recvd)
    nz = {s: sum(1 for o in order if o[1] == s) / chunks for s in '+-y'}
    return order, end, nz


def split(value):
    high = value.astype(jnp.bfloat16)
    return high, (value - high.astype(jnp.float32)).astype(jnp.bfloat16)


def dot(left, right):
    return jnp.dot(left, right, preferred_element_type=jnp.float32)


def dot_nt(left, right):
    return lax.dot_general(left, right, (((1,), (1,)), ((), ())), preferred_element_type=jnp.float32)


def dot_3(left_high, left_low, right_high, right_low):
    return dot(left_high, right_high) + (dot(left_high, right_low) + dot(left_low, right_high))


def shifted(rows, first_row, width):
    row = lax.broadcasted_iota(jnp.int32, rows.shape, 0) + first_row
    column = lax.broadcasted_iota(jnp.int32, rows.shape, 1)
    return jnp.where(row == column, 1.25, 0.0) - 0.25 * rows


def step_kernel(
    order,
    chunks,
    assign_hbm,
    newton_hbm,
    grad_hbm,
    stat_ref,
    moment_hbm,
    dir_ref,
    new_stat_ref,
    new_moment_ref,
    assign_ref,
    newton_ref,
    grad_ref,
    own_half,
    moment_ref,
    outgoing,
    block,
    block_turned,
    old,
    factor,
    core_grad,
    t_high,
    t_low,
    m_high,
    m_low,
    s_high,
    s_low,
    u_high,
    u_low,
    sent_root,
    other_root,
    quarter_ref,
    sums,
    own_direction,
    input_sem,
    output_sem,
    grad_send,
    grad_recv,
    pass_send,
    pass_recv,
    old_send,
    old_pass,
    old_recv,
    old_local,
    root_send,
    root_recv,
    sum_send,
    sum_recv,
    dir_send,
    dir_recv,
    dir_local,
):
    replica, fsdp = lax.axis_index("replica"), lax.axis_index("fsdp")
    z, y_high = replica // 2, lax.rem(replica, 2)
    chip, core = fsdp // 2, lax.rem(fsdp, 2)
    slot, side = chip // 2, lax.rem(chip, 2)
    member = lax.rem(fsdp, 4)
    twin = (replica, chip * 2 + 1 - core)
    beside = (replica, slot * 4 + (1 - side) * 2 + side)
    upward = (lax.rem(z + 1, 16) * 2 + y_high, fsdp)
    downward = (lax.rem(z + 15, 16) * 2 + y_high, fsdp)
    across = (z * 2 + 1 - y_high, fsdp)

    def same_core(distance):
        return (replica, lax.rem(chip + distance, 16) * 2 + core)

    def remote(source, target, send_sem, recv_sem, device):
        return pltpu.make_async_remote_copy(
            src_ref=source,
            dst_ref=target,
            send_sem=send_sem,
            recv_sem=recv_sem,
            device_id=device,
            device_id_type=MESH,
        )

    pairs = (
        (assign_hbm, assign_ref),
        (grad_hbm, grad_ref),
        (newton_hbm, newton_ref),
        (stat_ref.at[0], own_half),
        (moment_hbm.at[0], moment_ref),
    )
    inputs = [pltpu.make_async_copy(source, target, input_sem.at[i]) for i, (source, target) in enumerate(pairs)]
    for copy in inputs:
        copy.start()
    barrier = pltpu.get_barrier_semaphore()
    diagonal = (replica, slot * 4 + (1 - side) * 2 + (1 - core))
    greeted = [same_core(distance) for distance in range(1, 16)] + [twin, diagonal, upward, downward, across]
    for device in greeted:
        pl.semaphore_signal(barrier, inc=1, device_id=device, device_id_type=MESH)
    inputs[0].wait()
    inputs[1].wait()
    for target_slot in range(8):
        outgoing[target_slot] = grad_ref[lax.rem(assign_ref[target_slot], 8)]
    block[chip, core] = outgoing[slot]
    pl.semaphore_wait(barrier, len(greeted))

    grad_copies = []
    for distance in range(1, 16):
        target = lax.rem(chip + distance, 16)
        copy = remote(
            outgoing.at[target // 2],
            block.at[chip, core],
            grad_send.at[distance],
            grad_recv.at[distance],
            same_core(distance),
        )
        copy.start()
        grad_copies.append(copy)

    def old_piece(number):
        half, first, count, width, landing = OLD_PIECES[number]
        source = stat_ref.at[0, pl.ds(first, count), pl.ds(0, width)]
        here = old.at[pl.ds(landing, count), pl.ds(0, width)]
        return (
            half,
            remote(source, here, old_send.at[number], old_recv.at[number], beside),
            remote(source, here, old_pass.at[number], old_recv.at[number], twin),
            pltpu.make_async_copy(source, here, old_local.at[number]),
        )

    for number in range(4):
        half, to_beside, to_twin, to_self = old_piece(number)

        @pl.when(core == half)
        def _():
            to_beside.start()

        @pl.when((core == half) & (core == side))
        def _():
            to_self.start()

        @pl.when((core == half) & (core != side))
        def _():
            to_twin.start()

    pass_copies = []
    for distance in range(16):
        source = lax.rem(chip + 16 - distance, 16)
        if distance > 0:
            grad_copies[distance - 1].wait_recv()
        rows = block.at[source, core]
        copy = remote(rows, rows, pass_send.at[distance], pass_recv.at[distance], twin)
        copy.start()
        pass_copies.append(copy)
    for copy in pass_copies:
        copy.wait_recv()

    taken = assign_ref[slot]
    received = block[...].reshape(512, 512)
    row = lax.broadcasted_iota(jnp.int32, (512, 512), 0)
    column = lax.broadcasted_iota(jnp.int32, (512, 512), 1)
    identity = jnp.where(row == column, 1.0, 0.0).astype(jnp.bfloat16)
    flipped = dot_nt(identity, received)
    block_turned[...] = flipped.astype(jnp.bfloat16)

    def oriented(which):
        plain = block[...].reshape(512, 512)
        return jnp.where(lax.rem(taken // 8 + which, 2) == 1, block_turned[...], plain)

    core_grad[...] = oriented(core)
    grams = [dot_nt(core_grad[pl.ds(part * 256, 256), :], core_grad[...]) for part in range(2)]
    for number in range(4):
        half, to_beside, to_twin, to_self = old_piece(number)
        local = (core == half) & (core == side)

        @pl.when(local)
        def _():
            to_self.wait()

        @pl.when(jnp.logical_not(local))
        def _():
            to_beside.wait_recv()

    for first in (0, 512):
        old[pl.ds(first, 128), pl.ds(128, 128)] = old[pl.ds(first + 128, 128), pl.ds(0, 128)].T
    lower = old[256:512, :]
    quarters = ((old[0:256, :], lower.T), (lower, old[512:768, :]))
    squares = jnp.zeros((1, 1), jnp.float32)
    for part in range(2):
        rows = pl.ds(part * 256, 256)
        for half in range(2):
            entry = 0.9 * quarters[part][half] + 0.1 * grams[part][:, half * 256 : (half + 1) * 256]
            factor[rows, pl.ds(half * 256, 256)] = entry
            squares = squares + jnp.sum(entry * entry, keepdims=True)
    norm = jnp.sqrt(squares + 1e-06)
    inverse = 1.0 / norm
    scale = lax.rsqrt(jnp.sqrt(norm))

    for part in range(2):
        rows = pl.ds(part * 256, 256)
        iterate = factor[rows, :] * inverse
        m_high[rows, :], m_low[rows, :] = split(iterate)
        tangent = shifted(iterate, part * 256, 512)
        factor[rows, :] = tangent
        t_high[rows, :], t_low[rows, :] = split(tangent)
    for part in range(2):
        rows = pl.ds(part * 256, 256)
        s_high[rows, :], s_low[rows, :] = split(dot_3(t_high[rows, :], t_low[rows, :], t_high[...], t_low[...]))
    for part in range(2):
        rows = pl.ds(part * 256, 256)
        u_high[rows, :], u_low[rows, :] = split(dot_3(s_high[rows, :], s_low[rows, :], m_high[...], m_low[...]))
    for part in range(2):
        rows = pl.ds(part * 256, 256)
        iterate = dot_3(s_high[rows, :], s_low[rows, :], u_high[...], u_low[...])
        m_high[rows, :], m_low[rows, :] = split(iterate)
        t_high[rows, :], t_low[rows, :] = split(shifted(iterate, part * 256, 512))

    for part in range(2):
        rows = pl.ds(part * 256, 256)
        s_high[rows, :], s_low[rows, :] = split(dot_3(t_high[rows, :], t_low[rows, :], t_high[...], t_low[...]))
    inputs[2].wait()
    steps = newton_ref[lax.rem(taken, 8)]

    def root_rows(first):
        start = factor[pl.ds(pl.multiple_of(first * 256, 256), 256), :]
        second = dot_3(*split(start), t_high[...], t_low[...])
        third = dot_3(*split(second), m_high[...], m_low[...])
        third = dot_3(*split(third), s_high[...], s_low[...])
        third = dot_3(*split(third), s_high[...], s_low[...])
        third = 1.25 * second - 0.25 * third
        return scale * jnp.where(jnp.full((256, 512), steps) > 2, third, second)

    own = core * (1 - side)
    sent_root[...] = root_rows(1 - own)
    root_copy = remote(sent_root, other_root, root_send, root_recv, twin)
    root_copy.start()
    root_high, root_low = split(root_rows(own))
    shaped = dot(root_high, core_grad[...]) + dot(root_low, core_grad[...])
    u_high[0:256, :], u_low[0:256, :] = split(shaped)

    first_row = pl.multiple_of(own * 256, 256)
    first_column = pl.multiple_of((side * (1 - core) + core) * 256, 256)
    quarter_ref[...] = core_grad[pl.ds(first_row, 256), pl.ds(first_column, 256)].astype(jnp.float32)

    @pl.when(core == 1)
    def _():
        quarter_ref[...] = quarter_ref[...].T

    inputs[4].wait()
    entries = quarter_ref[...]
    fresh = 0.95 * moment_ref[...] + 0.05 * entries * entries
    moment_ref[...] = fresh
    adam = entries / (jnp.sqrt(fresh) + 1e-08)
    adam_sum = jnp.sum(adam * adam, keepdims=True)
    moment_out = pltpu.make_async_copy(moment_ref, new_moment_ref.at[0], output_sem.at[0])
    moment_out.start()
    root_copy.wait_recv()
    root_high, root_low = split(other_root[...])
    shaped_high, shaped_low = u_high[0:256, :], u_low[0:256, :]
    quarter = dot_nt(shaped_high, root_high) + (dot_nt(shaped_high, root_low) + dot_nt(shaped_low, root_high))
    quarter_ref[...] = quarter
    quarter_sum = jnp.sum(quarter * quarter, keepdims=True)
    line = lax.broadcasted_iota(jnp.int32, (8, 128), 0)
    sums[member] = jnp.where(line == 0, adam_sum, quarter_sum)
    sum_copies = []
    for distance in range(1, 4):
        device = (replica, slot * 4 + lax.rem(member + distance, 4))
        copy = remote(sums.at[member], sums.at[member], sum_send.at[distance], sum_recv.at[distance], device)
        copy.start()
        sum_copies.append(copy)

    @pl.when(core == 1)
    def _():
        quarter_ref[...] = quarter_ref[...].T

    for copy in sum_copies:
        copy.wait_recv()
    total = (sums[0] + sums[1]) + (sums[2] + sums[3])
    mean = total * (1.0 / (512 * 512))
    graft = jnp.sqrt(mean[0:1, 0:1]) / jnp.sqrt(mean[1:2, 0:1] + 1e-12)
    own_direction[...] = (graft * quarter_ref[...]).astype(jnp.bfloat16)

    keep = pltpu.make_async_copy(own_direction, dir_ref.at[replica, 0], dir_local)
    keep.start()
    height = 256 // chunks
    numbers = {send[3]: number for number, send in enumerate(order)}
    ways = {"+": upward, "-": downward, "y": across}

    def place(item):
        kind, distance, chunk = item
        column_of = y_high if kind == 0 else 1 - y_high
        return dir_ref.at[lax.rem(z + 16 - distance, 16) * 2 + column_of, 0, pl.ds(chunk * height, height), :]

    arrived = {(0, 0, chunk) for chunk in range(chunks)}

    def await_item(item):
        if item not in arrived:
            arrived.add(item)
            remote(place(item), place(item), dir_send.at[0], dir_recv.at[numbers[item]], upward).wait_recv()

    dir_copies = []
    stat_out = pltpu.make_async_copy(own_half, new_stat_ref.at[0], output_sem.at[1])
    placed = False
    for number, (_, way, item, landing) in enumerate(order):
        if not placed and item not in arrived:
            placed = True
            inputs[3].wait()
            block_turned[...] = oriented(side)
            half_rows = block_turned[pl.ds(pl.multiple_of(core * 256, 256), 256), :]
            own_half[...] = 0.9 * own_half[...] + 0.1 * dot_nt(block_turned[...], half_rows)
            stat_out.start()
        await_item(item)
        source = place(item)
        if item[:2] == (0, 0):
            source = own_direction.at[pl.ds(item[2] * height, height), :]
        copy = remote(source, place(item), dir_send.at[number], dir_recv.at[number], ways[way])
        copy.start()
        dir_copies.append(copy)
    for item in numbers:
        await_item(item)
    keep.wait()
    moment_out.wait()
    stat_out.wait()
    root_copy.wait_send()
    for number in range(4):
        half, to_beside, to_twin, to_self = old_piece(number)

        @pl.when(core == half)
        def _():
            to_beside.wait_send()

        @pl.when((core == half) & (core != side))
        def _():
            to_twin.wait_send()

    for copy in grad_copies + pass_copies + sum_copies + dir_copies:
        copy.wait_send()


OLD_PIECES = ((0, 128, 384, 256, 128), (1, 384, 128, 256, 640), (0, 0, 128, 128, 0), (1, 256, 128, 128, 512))
CROSSINGS = (0, 3, 6, -6, -3)
CHUNKS = 2


def place_kernel(dir_ref, stat_ref, moment_ref, dir_out, stat_out, moment_out, sem):
    copies = [
        pltpu.make_async_copy(dir_ref.at[pl.ds(part * 8, 8)], dir_out.at[pl.ds(part * 8, 8)], sem.at[part])
        for part in range(4)
    ]
    copies.append(pltpu.make_async_copy(stat_ref, stat_out, sem.at[4]))
    copies.append(pltpu.make_async_copy(moment_ref, moment_out, sem.at[5]))
    for copy in copies:
        copy.start()
    for copy in copies:
        copy.wait()


def on_device(grad, statistics, moment, assignment, newton_steps):
    order = make_plan(CROSSINGS, CHUNKS)[0]
    anywhere = pl.BlockSpec(memory_space=pl.ANY)
    wide_16 = pltpu.VMEM((512, 512), jnp.bfloat16)
    wide_32 = pltpu.VMEM((512, 512), jnp.float32)
    dma = pltpu.SemaphoreType.DMA
    results = pl.pallas_call(
        functools.partial(step_kernel, order, CHUNKS),
        out_shape=(
            jax.ShapeDtypeStruct((32, 1, 256, 256), jnp.bfloat16),
            jax.ShapeDtypeStruct((1, 512, 256), jnp.float32),
            jax.ShapeDtypeStruct((1, 256, 256), jnp.float32),
        ),
        in_specs=[anywhere] * 5,
        out_specs=(anywhere, anywhere, anywhere),
        scratch_shapes=[
            pltpu.SMEM((8,), jnp.int32),
            pltpu.SMEM((8,), jnp.int32),
            pltpu.VMEM((8, 16, 512), jnp.bfloat16),
            pltpu.VMEM((512, 256), jnp.float32),
            pltpu.VMEM((256, 256), jnp.float32),
            pltpu.VMEM((8, 16, 512), jnp.bfloat16),
            pltpu.VMEM((16, 2, 16, 512), jnp.bfloat16),
            wide_16,
            pltpu.VMEM((768, 256), jnp.float32),
            wide_32,
        ]
        + [wide_16] * 9
        + [
            pltpu.VMEM((256, 512), jnp.float32),
            pltpu.VMEM((256, 512), jnp.float32),
            pltpu.VMEM((256, 256), jnp.float32),
            pltpu.VMEM((4, 8, 128), jnp.float32),
            pltpu.VMEM((256, 256), jnp.bfloat16),
            dma((5,)),
            dma((2,)),
            dma((16,)),
            dma((16,)),
            dma((16,)),
            dma((16,)),
            dma((4,)),
            dma((4,)),
            dma((4,)),
            dma((4,)),
            dma,
            dma,
            dma((4,)),
            dma((4,)),
            dma((len(order),)),
            dma((len(order),)),
            dma,
        ],
        compiler_params=pltpu.CompilerParams(
            collective_id=0, has_side_effects=True, vmem_limit_bytes=24 << 20
        ),
        name="shampoo_step",
    )(*(pltpu.with_memory_space_constraint(x, pltpu.HBM) for x in (assignment, newton_steps, grad, statistics, moment)))
    return pl.pallas_call(
        place_kernel,
        out_shape=tuple(jax.ShapeDtypeStruct(result.shape, result.dtype) for result in results),
        in_specs=[anywhere] * 3,
        out_specs=[anywhere] * 3,
        scratch_shapes=[dma((6,))],
        compiler_params=pltpu.CompilerParams(vmem_limit_bytes=8 << 20),
        name="place_results",
    )(*results)


def solution(mesh):
    placed = (
        P("replica", "fsdp", None),
        P(("replica", "fsdp"), None, None),
        P(("replica", "fsdp"), None, None),
        P("replica"),
        P("replica"),
    )
    return jax.shard_map(
        on_device,
        mesh=mesh,
        in_specs=placed,
        out_specs=(
            P(None, "fsdp", None, None),
            P(("replica", "fsdp"), None, None),
            P(("replica", "fsdp"), None, None),
        ),
        check_vma=False,
    )
```

```python
import functools

import jax
import jax.numpy as jnp
from jax import lax
from jax.experimental import pallas as pl
from jax.experimental.pallas import tpu as pltpu
from jax.sharding import PartitionSpec as P

MESH = pl.DeviceIdType.MESH


def make_plan(cross, chunks, tz=2.95, ty=6.2, lz=1.6, ly=2.6):
    routes = {}
    def add(a, s, b): routes.setdefault(a, []).append((s, b))
    def norm(d): return d if d <= 8 else d - 16
    half = chunks // 2
    for c in range(chunks):
        for d in range(0, 7): add((0, d, c), '+', (0, d + 1, c))
        for d in range(0, -7, -1): add((0, d, c), '-', (0, d - 1, c))
        if c < half: add((0, 7, c), '+', (0, 8, c))
        else: add((0, -7, c), '-', (0, 8, c))
        for d in cross: add((0, d, c), 'y', (1, d, c))
        cs = sorted(x % 16 for x in cross)
        flip = 0
        for i, a in enumerate(cs):
            b = cs[(i + 1) % len(cs)]
            if b <= a: b += 16
            n = b - a - 1
            left = n // 2; right = n // 2
            if n % 2:
                if (c < half) : left += 1
                else: right += 1
            for j in range(left): add((1, norm((a + j) % 16), c), '+', (1, norm((a + j + 1) % 16), c))
            for j in range(right): add((1, norm((b - j) % 16), c), '-', (1, norm((b - j - 1) % 16), c))
    import functools
    cost = {'+': tz / chunks + lz, '-': tz / chunks + lz, 'y': ty / chunks + ly}
    @functools.lru_cache(None)
    def rem(item):
        return max([cost[s] + rem(b) for s, b in routes.get(item, [])], default=0)
    dur = {'+': tz / chunks, '-': tz / chunks, 'y': ty / chunks}
    lat = {'+': lz, '-': lz, 'y': ly}
    free = {'+': 0., '-': 0., 'y': 0.}
    ready = {'+': [], '-': [], 'y': []}
    def arrive(item, t):
        for s, b in routes.get(item, []):
            ready[s].append((t, item, b))
    for c in range(chunks): arrive((0, 0, c), 0.0)
    order = []; end = 0
    while any(ready.values()):
        best = None
        for s in ready:
            if not ready[s]: continue
            t = max(free[s], min(r[0] for r in ready[s]))
            if best is None or t < best[0]: best = (t, s)
        t, s = best
        cand = [r for r in ready[s] if r[0] <= t + 1e-9]
        cand.sort(key=lambda r: (-(cost[s] + rem(r[2])), r[0], r[1]))
        r = cand[0]; ready[s].remove(r)
        free[s] = t + dur[s]
        order.append((t, s, r[1], r[2]))
        ta = t + dur[s] + lat[s]
        end = max(end, ta)
        arrive(r[2], ta)
    recvd = {}
    for t, s, a, b in order:
        assert b not in recvd, b
        recvd[b] = 1
    assert len(recvd) == 31 * chunks, len(recvd)
    nz = {s: sum(1 for o in order if o[1] == s) / chunks for s in '+-y'}
    return order, end, nz


def split(value):
    high = value.astype(jnp.bfloat16)
    return high, (value - high.astype(jnp.float32)).astype(jnp.bfloat16)


def dot(left, right):
    return jnp.dot(left, right, preferred_element_type=jnp.float32)


def dot_nt(left, right):
    return lax.dot_general(left, right, (((1,), (1,)), ((), ())), preferred_element_type=jnp.float32)


def dot_3(left_high, left_low, right_high, right_low):
    return dot(left_high, right_high) + (dot(left_high, right_low) + dot(left_low, right_high))


def shifted(rows, first_row, width):
    row = lax.broadcasted_iota(jnp.int32, rows.shape, 0) + first_row
    column = lax.broadcasted_iota(jnp.int32, rows.shape, 1)
    return jnp.where(row == column, 1.25, 0.0) - 0.25 * rows


def step_kernel(
    order,
    chunks,
    assign_hbm,
    newton_hbm,
    grad_hbm,
    stat_ref,
    moment_hbm,
    dir_ref,
    new_stat_ref,
    new_moment_ref,
    assign_ref,
    newton_ref,
    grad_ref,
    own_half,
    moment_ref,
    outgoing,
    block,
    block_turned,
    old,
    factor,
    core_grad,
    t_high,
    t_low,
    m_high,
    m_low,
    s_high,
    s_low,
    u_high,
    u_low,
    sent_root,
    other_root,
    quarter_ref,
    sums,
    own_direction,
    input_sem,
    output_sem,
    grad_send,
    grad_recv,
    pass_send,
    pass_recv,
    old_send,
    old_pass,
    old_recv,
    old_local,
    root_send,
    root_recv,
    sum_send,
    sum_recv,
    dir_send,
    dir_recv,
    dir_local,
):
    replica, fsdp = lax.axis_index("replica"), lax.axis_index("fsdp")
    z, y_high = replica // 2, lax.rem(replica, 2)
    chip, core = fsdp // 2, lax.rem(fsdp, 2)
    slot, side = chip // 2, lax.rem(chip, 2)
    member = lax.rem(fsdp, 4)
    twin = (replica, chip * 2 + 1 - core)
    beside = (replica, slot * 4 + (1 - side) * 2 + side)
    upward = (lax.rem(z + 1, 16) * 2 + y_high, fsdp)
    downward = (lax.rem(z + 15, 16) * 2 + y_high, fsdp)
    across = (z * 2 + 1 - y_high, fsdp)

    def same_core(distance):
        return (replica, lax.rem(chip + distance, 16) * 2 + core)

    def remote(source, target, send_sem, recv_sem, device):
        return pltpu.make_async_remote_copy(
            src_ref=source,
            dst_ref=target,
            send_sem=send_sem,
            recv_sem=recv_sem,
            device_id=device,
            device_id_type=MESH,
        )

    pairs = (
        (assign_hbm, assign_ref),
        (grad_hbm, grad_ref),
        (newton_hbm, newton_ref),
        (stat_ref.at[0], own_half),
        (moment_hbm.at[0], moment_ref),
    )
    inputs = [pltpu.make_async_copy(source, target, input_sem.at[i]) for i, (source, target) in enumerate(pairs)]
    for copy in inputs:
        copy.start()
    barrier = pltpu.get_barrier_semaphore()
    diagonal = (replica, slot * 4 + (1 - side) * 2 + (1 - core))
    greeted = [same_core(distance) for distance in range(1, 16)] + [twin, diagonal, upward, downward, across]
    for device in greeted:
        pl.semaphore_signal(barrier, inc=1, device_id=device, device_id_type=MESH)
    row = lax.broadcasted_iota(jnp.int32, (512, 512), 0)
    column = lax.broadcasted_iota(jnp.int32, (512, 512), 1)
    t_high[...] = jnp.where(row == column, 1.0, 0.0).astype(jnp.bfloat16)
    inputs[0].wait()
    inputs[1].wait()
    for target_slot in range(8):
        outgoing[target_slot] = grad_ref[lax.rem(assign_ref[target_slot], 8)]
    block[chip, core] = outgoing[slot]
    pl.semaphore_wait(barrier, len(greeted))

    grad_copies = []
    for distance in range(1, 16):
        target = lax.rem(chip + distance, 16)
        copy = remote(
            outgoing.at[target // 2],
            block.at[chip, core],
            grad_send.at[distance],
            grad_recv.at[distance],
            same_core(distance),
        )
        copy.start()
        grad_copies.append(copy)

    def old_piece(number):
        half, first, count, width, landing = OLD_PIECES[number]
        source = stat_ref.at[0, pl.ds(first, count), pl.ds(0, width)]
        here = old.at[pl.ds(landing, count), pl.ds(0, width)]
        return (
            half,
            remote(source, here, old_send.at[number], old_recv.at[number], beside),
            remote(source, here, old_pass.at[number], old_recv.at[number], twin),
            pltpu.make_async_copy(source, here, old_local.at[number]),
        )

    for number in range(4):
        half, to_beside, to_twin, to_self = old_piece(number)

        @pl.when(core == half)
        def _():
            to_beside.start()

        @pl.when((core == half) & (core == side))
        def _():
            to_self.start()

        @pl.when((core == half) & (core != side))
        def _():
            to_twin.start()

    pass_copies = []
    for distance in range(16):
        source = lax.rem(chip + 16 - distance, 16)
        if distance > 0:
            grad_copies[distance - 1].wait_recv()
        rows = block.at[source, core]
        copy = remote(rows, rows, pass_send.at[distance], pass_recv.at[distance], twin)
        copy.start()
        pass_copies.append(copy)
    for copy in pass_copies:
        copy.wait_recv()

    taken = assign_ref[slot]
    received = block[...].reshape(512, 512)
    flipped = dot_nt(t_high[...], received)
    block_turned[...] = flipped.astype(jnp.bfloat16)

    def oriented(which):
        plain = block[...].reshape(512, 512)
        return jnp.where(lax.rem(taken // 8 + which, 2) == 1, block_turned[...], plain)

    core_grad[...] = oriented(core)
    grams = [dot_nt(core_grad[pl.ds(part * 256, 256), :], core_grad[...]) for part in range(2)]
    for number in range(4):
        half, to_beside, to_twin, to_self = old_piece(number)
        local = (core == half) & (core == side)

        @pl.when(local)
        def _():
            to_self.wait()

        @pl.when(jnp.logical_not(local))
        def _():
            to_beside.wait_recv()

    for first in (0, 512):
        old[pl.ds(first, 128), pl.ds(128, 128)] = old[pl.ds(first + 128, 128), pl.ds(0, 128)].T
    lower = old[256:512, :]
    quarters = ((old[0:256, :], lower.T), (lower, old[512:768, :]))
    squares = jnp.zeros((1, 1), jnp.float32)
    for part in range(2):
        rows = pl.ds(part * 256, 256)
        for half in range(2):
            entry = 0.9 * quarters[part][half] + 0.1 * grams[part][:, half * 256 : (half + 1) * 256]
            factor[rows, pl.ds(half * 256, 256)] = entry
            squares = squares + jnp.sum(entry * entry, keepdims=True)
    norm = jnp.sqrt(squares + 1e-06)
    inverse = 1.0 / norm
    scale = lax.rsqrt(jnp.sqrt(norm))

    for part in range(2):
        rows = pl.ds(part * 256, 256)
        iterate = factor[rows, :] * inverse
        m_high[rows, :], m_low[rows, :] = split(iterate)
        tangent = shifted(iterate, part * 256, 512)
        factor[rows, :] = tangent
        t_high[rows, :], t_low[rows, :] = split(tangent)
    for part in range(2):
        rows = pl.ds(part * 256, 256)
        s_high[rows, :], s_low[rows, :] = split(dot_3(t_high[rows, :], t_low[rows, :], t_high[...], t_low[...]))
    for part in range(2):
        rows = pl.ds(part * 256, 256)
        u_high[rows, :], u_low[rows, :] = split(dot_3(s_high[rows, :], s_low[rows, :], m_high[...], m_low[...]))
    for part in range(2):
        rows = pl.ds(part * 256, 256)
        iterate = dot_3(s_high[rows, :], s_low[rows, :], u_high[...], u_low[...])
        m_high[rows, :], m_low[rows, :] = split(iterate)
        t_high[rows, :], t_low[rows, :] = split(shifted(iterate, part * 256, 512))

    for part in range(2):
        rows = pl.ds(part * 256, 256)
        s_high[rows, :], s_low[rows, :] = split(dot_3(t_high[rows, :], t_low[rows, :], t_high[...], t_low[...]))
    inputs[2].wait()
    steps = newton_ref[lax.rem(taken, 8)]

    def root_rows(first):
        start = factor[pl.ds(pl.multiple_of(first * 256, 256), 256), :]
        second = dot_3(*split(start), t_high[...], t_low[...])
        third = dot_3(*split(second), m_high[...], m_low[...])
        third = dot_3(*split(third), s_high[...], s_low[...])
        third = dot_3(*split(third), s_high[...], s_low[...])
        third = 1.25 * second - 0.25 * third
        return scale * jnp.where(jnp.full((256, 512), steps) > 2, third, second)

    own = core * (1 - side)
    sent_root[...] = root_rows(1 - own)
    root_copy = remote(sent_root, other_root, root_send, root_recv, twin)
    root_copy.start()
    root_high, root_low = split(root_rows(own))
    shaped = dot(root_high, core_grad[...]) + dot(root_low, core_grad[...])
    u_high[0:256, :], u_low[0:256, :] = split(shaped)

    first_row = pl.multiple_of(own * 256, 256)
    first_column = pl.multiple_of((side * (1 - core) + core) * 256, 256)
    quarter_ref[...] = core_grad[pl.ds(first_row, 256), pl.ds(first_column, 256)].astype(jnp.float32)

    @pl.when(core == 1)
    def _():
        quarter_ref[...] = quarter_ref[...].T

    inputs[4].wait()
    entries = quarter_ref[...]
    fresh = 0.95 * moment_ref[...] + 0.05 * entries * entries
    moment_ref[...] = fresh
    adam = entries / (jnp.sqrt(fresh) + 1e-08)
    adam_sum = jnp.sum(adam * adam, keepdims=True)
    moment_out = pltpu.make_async_copy(moment_ref, new_moment_ref.at[0], output_sem.at[0])
    moment_out.start()
    root_copy.wait_recv()
    root_high, root_low = split(other_root[...])
    shaped_high, shaped_low = u_high[0:256, :], u_low[0:256, :]
    quarter = dot_nt(shaped_high, root_high) + (dot_nt(shaped_high, root_low) + dot_nt(shaped_low, root_high))
    quarter_ref[...] = quarter
    quarter_sum = jnp.sum(quarter * quarter, keepdims=True)
    line = lax.broadcasted_iota(jnp.int32, (8, 128), 0)
    sums[member] = jnp.where(line == 0, adam_sum, quarter_sum)
    sum_copies = []
    for distance in range(1, 4):
        device = (replica, slot * 4 + lax.rem(member + distance, 4))
        copy = remote(sums.at[member], sums.at[member], sum_send.at[distance], sum_recv.at[distance], device)
        copy.start()
        sum_copies.append(copy)

    @pl.when(core == 1)
    def _():
        quarter_ref[...] = quarter_ref[...].T

    for copy in sum_copies:
        copy.wait_recv()
    total = (sums[0] + sums[1]) + (sums[2] + sums[3])
    mean = total * (1.0 / (512 * 512))
    graft = jnp.sqrt(mean[0:1, 0:1]) / jnp.sqrt(mean[1:2, 0:1] + 1e-12)
    own_direction[...] = (graft * quarter_ref[...]).astype(jnp.bfloat16)

    keep = pltpu.make_async_copy(own_direction, dir_ref.at[replica, 0], dir_local)
    keep.start()
    height = 256 // chunks
    numbers = {send[3]: number for number, send in enumerate(order)}
    ways = {"+": upward, "-": downward, "y": across}

    def place(item):
        kind, distance, chunk = item
        column_of = y_high if kind == 0 else 1 - y_high
        return dir_ref.at[lax.rem(z + 16 - distance, 16) * 2 + column_of, 0, pl.ds(chunk * height, height), :]

    arrived = {(0, 0, chunk) for chunk in range(chunks)}

    def await_item(item):
        if item not in arrived:
            arrived.add(item)
            remote(place(item), place(item), dir_send.at[0], dir_recv.at[numbers[item]], upward).wait_recv()

    dir_copies = []
    stat_out = pltpu.make_async_copy(own_half, new_stat_ref.at[0], output_sem.at[1])
    placed = False
    for number, (_, way, item, landing) in enumerate(order):
        if not placed and item not in arrived:
            placed = True
            inputs[3].wait()
            block_turned[...] = oriented(side)
            half_rows = block_turned[pl.ds(pl.multiple_of(core * 256, 256), 256), :]
            own_half[...] = 0.9 * own_half[...] + 0.1 * dot_nt(block_turned[...], half_rows)
            stat_out.start()
        await_item(item)
        source = place(item)
        if item[:2] == (0, 0):
            source = own_direction.at[pl.ds(item[2] * height, height), :]
        copy = remote(source, place(item), dir_send.at[number], dir_recv.at[number], ways[way])
        copy.start()
        dir_copies.append(copy)
    for item in numbers:
        await_item(item)
    keep.wait()
    moment_out.wait()
    stat_out.wait()
    root_copy.wait_send()
    for number in range(4):
        half, to_beside, to_twin, to_self = old_piece(number)

        @pl.when(core == half)
        def _():
            to_beside.wait_send()

        @pl.when((core == half) & (core != side))
        def _():
            to_twin.wait_send()

    for copy in grad_copies + pass_copies + sum_copies + dir_copies:
        copy.wait_send()


OLD_PIECES = ((0, 128, 384, 256, 128), (1, 384, 128, 256, 640), (0, 0, 128, 128, 0), (1, 256, 128, 128, 512))
CROSSINGS = (0, 1, 4, -4, -1)
CHUNKS = 4


def place_kernel(dir_ref, stat_ref, moment_ref, dir_out, stat_out, moment_out, sem):
    copies = [
        pltpu.make_async_copy(dir_ref.at[pl.ds(part * 8, 8)], dir_out.at[pl.ds(part * 8, 8)], sem.at[part])
        for part in range(4)
    ]
    copies.append(pltpu.make_async_copy(stat_ref, stat_out, sem.at[4]))
    copies.append(pltpu.make_async_copy(moment_ref, moment_out, sem.at[5]))
    for copy in copies:
        copy.start()
    for copy in copies:
        copy.wait()


def on_device(grad, statistics, moment, assignment, newton_steps):
    order = make_plan(CROSSINGS, CHUNKS, tz=2.62, ty=6.2, lz=2.2, ly=4.0)[0]
    anywhere = pl.BlockSpec(memory_space=pl.ANY)
    wide_16 = pltpu.VMEM((512, 512), jnp.bfloat16)
    wide_32 = pltpu.VMEM((512, 512), jnp.float32)
    dma = pltpu.SemaphoreType.DMA
    results = pl.pallas_call(
        functools.partial(step_kernel, order, CHUNKS),
        out_shape=(
            jax.ShapeDtypeStruct((32, 1, 256, 256), jnp.bfloat16),
            jax.ShapeDtypeStruct((1, 512, 256), jnp.float32),
            jax.ShapeDtypeStruct((1, 256, 256), jnp.float32),
        ),
        in_specs=[anywhere] * 5,
        out_specs=(anywhere, anywhere, anywhere),
        scratch_shapes=[
            pltpu.SMEM((8,), jnp.int32),
            pltpu.SMEM((8,), jnp.int32),
            pltpu.VMEM((8, 16, 512), jnp.bfloat16),
            pltpu.VMEM((512, 256), jnp.float32),
            pltpu.VMEM((256, 256), jnp.float32),
            pltpu.VMEM((8, 16, 512), jnp.bfloat16),
            pltpu.VMEM((16, 2, 16, 512), jnp.bfloat16),
            wide_16,
            pltpu.VMEM((768, 256), jnp.float32),
            wide_32,
        ]
        + [wide_16] * 9
        + [
            pltpu.VMEM((256, 512), jnp.float32),
            pltpu.VMEM((256, 512), jnp.float32),
            pltpu.VMEM((256, 256), jnp.float32),
            pltpu.VMEM((4, 8, 128), jnp.float32),
            pltpu.VMEM((256, 256), jnp.bfloat16),
            dma((5,)),
            dma((2,)),
            dma((16,)),
            dma((16,)),
            dma((16,)),
            dma((16,)),
            dma((4,)),
            dma((4,)),
            dma((4,)),
            dma((4,)),
            dma,
            dma,
            dma((4,)),
            dma((4,)),
            dma((len(order),)),
            dma((len(order),)),
            dma,
        ],
        compiler_params=pltpu.CompilerParams(
            collective_id=0, has_side_effects=True, vmem_limit_bytes=24 << 20
        ),
        name="shampoo_step",
    )(*(pltpu.with_memory_space_constraint(x, pltpu.HBM) for x in (assignment, newton_steps, grad, statistics, moment)))
    return pl.pallas_call(
        place_kernel,
        out_shape=tuple(jax.ShapeDtypeStruct(result.shape, result.dtype) for result in results),
        in_specs=[anywhere] * 3,
        out_specs=[anywhere] * 3,
        scratch_shapes=[dma((6,))],
        compiler_params=pltpu.CompilerParams(vmem_limit_bytes=8 << 20),
        name="place_results",
    )(*results)


def solution(mesh):
    placed = (
        P("replica", "fsdp", None),
        P(("replica", "fsdp"), None, None),
        P(("replica", "fsdp"), None, None),
        P("replica"),
        P("replica"),
    )
    return jax.shard_map(
        on_device,
        mesh=mesh,
        in_specs=placed,
        out_specs=(
            P(None, "fsdp", None, None),
            P(("replica", "fsdp"), None, None),
            P(("replica", "fsdp"), None, None),
        ),
        check_vma=False,
    )
```
